32 devices in a mesh: section: 2 (over x), dp: 4 (over y, core), tensor: 4 (over z).
Axes of the slice: x: 2, y: 2, z: 4, core: 2. Of those that a mesh axis runs over, the one named last changes fastest.
Arguments:
- inputs: bfloat16 [2, 2048, 4, 768], P(None, 'tensor', 'dp'), may hold values from -6 to 6
- segments: int32 [2, 4, 2048], P(None, 'dp'), may hold values from 0 to 2, as said below
- w_qkv: bfloat16 [2, 768, 3, 768], P('section', 'dp', None, 'tensor'), may hold values from -0.21875 to 0.21875
- qv_bias: bfloat16 [2, 2, 12, 64], P('section', None, 'tensor', 'dp'), may hold values from -3 to 3
- w_out: bfloat16 [2, 768, 768], P('section', 'tensor', 'dp'), may hold values from -3.5 to 3.5
- w_up: bfloat16 [2, 768, 3072], P('section', 'dp', 'tensor'), may hold values from -0.21875 to 0.21875
- up_bias: bfloat16 [2, 24, 128], P('section', 'tensor', 'dp'), may hold values from -3 to 3
- w_down: bfloat16 [2, 3072, 768], P('section', 'tensor', 'dp'), may hold values from -0.109375 to 0.109375
- norm_gains: bfloat16 [2, 2, 768], P('section', None, ('dp', 'tensor')), may hold values from 0.099609375 to 1.8984375
- offsets: bfloat16 [2, 4, 768], P('section', None, ('dp', 'tensor')), may hold values from -3 to 3
- cotangent: bfloat16 [2, 2048, 4, 768], P(None, 'tensor', 'dp'), may hold values from -6 to 6
Outputs:
- layer_outputs: bfloat16 [2, 2, 2048, 4, 768], P('section', None, 'tensor', 'dp')
- input_grads: float32 [2, 2, 2048, 4, 768], P('section', None, 'tensor', 'dp')
- grad_w_qkv: float32 [2, 768, 3, 768], P('section', 'dp', None, 'tensor')
- grad_qv_bias: float32 [2, 2, 12, 64], P('section', None, 'tensor', 'dp')
- grad_w_out: float32 [2, 768, 768], P('section', 'tensor', 'dp')
- grad_w_up: float32 [2, 768, 3072], P('section', 'dp', 'tensor')
- grad_up_bias: float32 [2, 24, 128], P('section', 'tensor', 'dp')
- grad_w_down: float32 [2, 3072, 768], P('section', 'tensor', 'dp')
- grad_norm_gains: float32 [2, 2, 768], P('section', None, ('dp', 'tensor'))
- grad_offsets: float32 [2, 4, 768], P('section', None, ('dp', 'tensor'))
The draws below stay inside these ranges and needn't reach their ends.
Inputs may be any that keep to these rules, and one draw needn't show every extreme that they name: Each packed row holds three segments numbered 0, 1, 2 in this order, each of one token or more; segment 1 begins in the first quarter of the row and ends in its last quarter.
All inputs are finite; a program needn't handle non-finite values.
Results may differ from the reference program's by a relative error of at most 0.02.
Values may be sent and summed in bfloat16 or wider, within the bound.
A program may use at most 256 MiB of HBM per device.

```python
import jax
import jax.numpy as jnp
from jax import lax

D = 768
H = 12
HD = 64
FF = 3072
L = 2048
MICRO = 2
ROWS = 4


def draw_segments(key, part):
    key = jax.random.fold_in(key, 7)
    first_key, second_key = jax.random.split(key)
    first_cut = jax.random.randint(first_key, (MICRO, ROWS, 1), 1, L // 4)
    second_cut = jax.random.randint(second_key, (MICRO, ROWS, 1), 3 * L // 4 + 1, L)
    positions = jnp.arange(L, dtype=jnp.int32)
    return (positions >= first_cut).astype(jnp.int32) + (positions >= second_cut).astype(jnp.int32)


def levels(rng, shape, cuts, low, high):
    gain = 1.0
    for dim, parts in cuts:
        steps = jax.random.uniform(jax.random.fold_in(jax.random.fold_in(rng, 6), dim), (parts,), jnp.float32, low / len(cuts), high / len(cuts))
        gain = gain * jnp.repeat(jnp.exp(steps), shape[dim] // parts).reshape((-1,) + (1,) * (len(shape) - 1 - dim))
    return gain


def gaussian(own_key, extent, deviation, reach, cuts=(), held_as=jnp.bfloat16):
    values = deviation * jax.random.normal(own_key, extent, jnp.float32)
    if cuts:
        values = values * levels(own_key, extent, cuts, -0.22, 0.18)
    return jnp.clip(values, -reach, reach).astype(held_as)


def setup_inputs(seed: int = 0) -> dict:
    streams_of = jax.random.split(jax.random.key(seed), 12)
    inputs = gaussian(streams_of[0], (MICRO, L, ROWS, D), 1.0, 6.0, ((1, 4), (2, 4)))
    segments = draw_segments(jax.random.fold_in(streams_of[11], 71), 0)
    w_qkv = gaussian(streams_of[2], (2, D, 3, D), D ** -0.5, 0.21875, ((0, 2), (1, 4), (3, 4)))
    qv_bias = gaussian(streams_of[3], (2, 2, H, HD), 0.5, 3.0, ((0, 2), (2, 4), (3, 4)))
    w_out = gaussian(streams_of[4], (2, D, D), (max(1, D // 256)) ** -0.5, 3.5, ((0, 2), (1, 4), (2, 4)))
    w_up = gaussian(streams_of[5], (2, D, FF), D ** -0.5, 0.21875, ((0, 2), (1, 4), (2, 4)))
    up_bias = gaussian(streams_of[6], (2, FF // 128, 128), 0.5, 3.0, ((0, 2), (1, 4), (2, 4)))
    w_down = gaussian(streams_of[7], (2, FF, D), FF ** -0.5, 0.109375, ((0, 2), (1, 4), (2, 4)))
    norm_gains = jnp.clip(1.0 + 0.18 * jax.random.normal(streams_of[8], (2, 2, D), jnp.float32), 0.099609375, 1.8984375).astype(jnp.bfloat16)
    offsets = gaussian(streams_of[9], (2, 4, D), 0.5, 3.0, ((0, 2), (2, 16)))
    cotangent = gaussian(streams_of[10], (MICRO, L, ROWS, D), 1.0, 6.0, ((1, 4), (2, 4)))
    return dict(inputs=inputs, segments=segments, w_qkv=w_qkv, qv_bias=qv_bias, w_out=w_out, w_up=w_up, up_bias=up_bias, w_down=w_down, norm_gains=norm_gains, offsets=offsets, cotangent=cotangent)


EPSILON = 1e-05
HIGH = lax.Precision.HIGHEST

@jax.custom_vjp
def low(v):
    return lax.optimization_barrier(v.astype(jnp.bfloat16)).astype(jnp.float32)

@jax.custom_vjp
def low_back(v):
    return v

def low_keep(v):
    return (low(v), None)

def low_pass(kept, grad):
    return (grad,)

def back_keep(v):
    return (v, None)

def back_low(kept, grad):
    return (low(grad),)
low.defvjp(low_keep, low_pass)
low_back.defvjp(back_keep, back_low)

def rounded(values):
    return low(low_back(values))

def layer_norm(inputs_row, norm_gain, norm_shift):
    centre = inputs_row - lax.optimization_barrier(jnp.mean(inputs_row, -1, keepdims=True))
    variance = lax.optimization_barrier(jnp.mean(centre * centre, -1, keepdims=True))
    return centre * lax.rsqrt(variance + EPSILON) * norm_gain + norm_shift

def attention(queries, key_rows, value_rows, segment_ids):
    length_all = queries.shape[0]
    block_size = min(512, length_all)
    block_count = length_all // block_size
    score_scale = HD ** (-0.5)
    positions = jnp.arange(length_all, dtype=jnp.int32)

    def one_block(operands):
        query_block, segment_block, position_block = operands
        scores = low_back(jnp.einsum('qhe,khe->hqk', query_block, key_rows, precision=HIGH) * score_scale)
        allowed = (positions[None, :] <= position_block[:, None]) & (segment_ids[None, :] == segment_block[:, None])
        masked = jnp.where(allowed[None], scores, -1e+30)
        exponent = jnp.exp(masked - lax.optimization_barrier(jnp.max(masked, -1, keepdims=True)))
        weights = low(exponent / lax.optimization_barrier(jnp.sum(exponent, -1, keepdims=True)))
        return jnp.einsum('hqk,khe->qhe', weights, value_rows, precision=HIGH)
    outputs = lax.map(jax.checkpoint(one_block), (queries.reshape(block_count, block_size, H, HD), segment_ids.reshape(block_count, block_size), positions.reshape(block_count, block_size)))
    return outputs.reshape(length_all, D)

def decoder_layer(inputs_row, segment_ids, weights_set):
    w_attn, attn_bias, w_proj, w_hidden, hidden_bias, w_back, gains_pair, offsets_set = weights_set
    length_all = inputs_row.shape[0]
    normed_one = low(layer_norm(inputs_row, gains_pair[0], offsets_set[0]))
    projected = jnp.einsum('ld,dcf->lcf', normed_one, w_attn, precision=HIGH)
    queries = rounded(projected[:, 0] + attn_bias[0].reshape(D))
    key_rows = rounded(projected[:, 1])
    value_rows = rounded(projected[:, 2] + attn_bias[1].reshape(D))
    mixed = rounded(attention(queries.reshape(length_all, H, HD), key_rows.reshape(length_all, H, HD), value_rows.reshape(length_all, H, HD), segment_ids))
    branch = low_back(jnp.dot(mixed, w_proj, precision=HIGH) + offsets_set[1])
    after_attn = inputs_row + branch
    normed_two = low(layer_norm(after_attn, gains_pair[1], offsets_set[2]))
    pre_act = low_back(jnp.dot(normed_two, w_hidden, precision=HIGH) + hidden_bias)
    activated = low(jax.nn.gelu(pre_act, approximate=True))
    return after_attn + low_back(jnp.dot(activated, w_back, precision=HIGH) + offsets_set[3])

def reference(inputs, segments, w_qkv, qv_bias, w_out, w_up, up_bias, w_down, norm_gains, offsets, cotangent):
    weights_all = (w_qkv.astype(jnp.float32), qv_bias.astype(jnp.float32), w_out.astype(jnp.float32), w_up.astype(jnp.float32), up_bias.astype(jnp.float32).reshape(2, FF), w_down.astype(jnp.float32), norm_gains.astype(jnp.float32), offsets.astype(jnp.float32))
    flat_inputs = inputs.astype(jnp.float32).transpose(0, 2, 1, 3).reshape(MICRO * ROWS, L, D)
    flat_cot = cotangent.astype(jnp.float32).transpose(0, 2, 1, 3).reshape(MICRO * ROWS, L, D)
    flat_segments = segments.reshape(MICRO * ROWS, L)

    def one_row(totals, operands):
        row_input, row_segments, row_cot = operands

        def sections(first_input, mid_offset, weights_now):
            first_layer = tuple((weight_pair[0] for weight_pair in weights_now))
            second_layer = tuple((weight_pair[1] for weight_pair in weights_now))
            first_out = decoder_layer(first_input, row_segments, first_layer)
            second_out = decoder_layer(low(first_out) + mid_offset, row_segments, second_layer)
            return (second_out, (first_out, second_out))
        _, pullback, outs_pair = jax.vjp(sections, row_input, jnp.zeros_like(row_input), weights_all, has_aux=True)
        grad_input, grad_mid, grad_weights = pullback(row_cot)
        totals = jax.tree.map(lambda left_sum, right_sum: left_sum + right_sum, totals, grad_weights)
        return (totals, (outs_pair[0], outs_pair[1], grad_input, grad_mid))
    start_totals = jax.tree.map(jnp.zeros_like, weights_all)
    totals, collected = lax.scan(one_row, start_totals, (flat_inputs, flat_segments, flat_cot))

    def arrange(pair_first, pair_second):
        return jnp.stack([pair_first, pair_second]).reshape(2, MICRO, ROWS, L, D).transpose(0, 1, 3, 2, 4)
    layer_outputs = arrange(collected[0], collected[1]).astype(jnp.bfloat16)
    input_grads = arrange(collected[2], collected[3])
    return (layer_outputs, input_grads, totals[0], totals[1], totals[2], totals[3], totals[4].reshape(2, FF // 128, 128), totals[5], totals[6], totals[7])
```

```python
import jax
import jax.numpy as jnp
from jax import lax
from jax.sharding import Mesh, PartitionSpec as P

EPSILON = 1e-05
GROUP = ("section", "core")
REPLICAS = ("outer", "tensor")
EXCHANGE = ("section", "core", "tensor")
EVERY = ("section", "outer", "core", "tensor")
BF = jnp.bfloat16
F32 = jnp.float32


def dot(left, right, contract):
    return lax.dot_general(left, right, ((contract[0], contract[1]), ((), ())), preferred_element_type=F32)


def sizes():
    return lax.axis_size("section"), lax.axis_size("core"), lax.axis_size("tensor")


def place(section, core, tensor):
    _, cores, tensors = sizes()
    return (section * cores + core) * tensors + tensor


def to_sequence(value):
    sections, cores, tensors = sizes()
    route = [
        (place(a, b, e), place(e // cores, e % cores, b * sections + a))
        for a in range(sections)
        for b in range(cores)
        for e in range(tensors)
    ]
    return lax.ppermute(value, EXCHANGE, route)


def from_sequence(value, layer, part):
    sections, cores, tensors = sizes()
    route = [
        (place(e // cores, e % cores, b * sections + part), place(layer, b, e))
        for b in range(cores)
        for e in range(tensors)
    ]
    return lax.ppermute(value, EXCHANGE, route)


def both_parts(value, layer):
    return [from_sequence(value, layer, part) for part in range(lax.axis_size("section"))]


def norm_forward(hidden_in, norm_gain, norm_shift):
    mean_value = jnp.mean(hidden_in, -1, keepdims=True)
    centred = hidden_in - mean_value
    variance = jnp.mean(centred * centred, -1, keepdims=True)
    inverse = lax.rsqrt(variance + EPSILON)
    normed = centred * inverse
    return (normed * norm_gain + norm_shift, normed, inverse)


def norm_backward(gradient, norm_gain, normed, inverse):
    scaled = gradient * norm_gain
    result = inverse * (
        scaled
        - jnp.mean(scaled, -1, keepdims=True)
        - normed * jnp.mean(scaled * normed, -1, keepdims=True)
    )
    return (result, jnp.sum(gradient * normed, axis=0), jnp.sum(gradient, axis=0))


def gather_rows(values):
    return lax.all_gather(values, GROUP, axis=0, tiled=True)


def reduce_rows(values):
    return lax.psum_scatter(values.astype(BF), GROUP, scatter_dimension=0, tiled=True).astype(F32)


def block_of(length_all):
    return min(512, length_all)


def block_scores(queries, key_rows, segment_ids, start, stop, score_scale):
    scores = (
        jnp.einsum("qhe,khe->hqk", queries[start:stop], key_rows[:stop], preferred_element_type=F32)
        * score_scale
    )
    allowed = (
        jnp.arange(stop, dtype=jnp.int32)[None, :]
        <= jnp.arange(start, stop, dtype=jnp.int32)[:, None]
    ) & (segment_ids[None, :stop] == segment_ids[start:stop, None])
    return scores, allowed[None]


def attend_forward(queries, key_rows, value_rows, segment_ids):
    length_all, head_count, head_width = queries.shape
    block = block_of(length_all)
    outs, logs = [], []
    for start in range(0, length_all, block):
        stop = start + block
        scores, allowed = block_scores(
            queries, key_rows, segment_ids, start, stop, head_width ** (-0.5)
        )
        masked = jnp.where(allowed, scores, -1e30)
        row_peak = jnp.max(masked, -1, keepdims=True)
        exponent = jnp.exp(masked - row_peak)
        weight_sum = jnp.sum(exponent, -1, keepdims=True)
        probabilities = (exponent / weight_sum).astype(BF)
        output = jnp.einsum(
            "hqk,khe->qhe", probabilities, value_rows[:stop], preferred_element_type=F32
        )
        outs.append(output.astype(BF))
        logs.append(row_peak + jnp.log(weight_sum))
    return jnp.concatenate(outs).reshape(length_all, -1), logs


def attend_backward(queries, key_rows, value_rows, segment_ids, logs, grad_mixed):
    length_all, head_count, head_width = queries.shape
    block = block_of(length_all)
    score_scale = head_width ** (-0.5)
    grad_q = []
    grad_k = jnp.zeros(key_rows.shape, F32)
    grad_v = jnp.zeros(key_rows.shape, F32)
    for index, start in enumerate(range(0, length_all, block)):
        stop = start + block
        scores, allowed = block_scores(queries, key_rows, segment_ids, start, stop, score_scale)
        grad_block = grad_mixed[start:stop]
        probabilities = jnp.where(allowed, jnp.exp(scores - logs[index]), 0.0)
        grad_v = grad_v.at[:stop].add(
            jnp.einsum(
                "hqk,qhe->khe", probabilities.astype(BF), grad_block, preferred_element_type=F32
            )
        )
        grad_probs = jnp.einsum(
            "qhe,khe->hqk", grad_block, value_rows[:stop], preferred_element_type=F32
        )
        inner_sum = jnp.sum(probabilities * grad_probs, -1, keepdims=True)
        grad_scores = (probabilities * (grad_probs - inner_sum)).astype(BF)
        grad_q.append(
            (
                jnp.einsum("hqk,khe->qhe", grad_scores, key_rows[:stop], preferred_element_type=F32)
                * score_scale
            ).astype(BF)
        )
        grad_k = grad_k.at[:stop].add(
            jnp.einsum("hqk,qhe->khe", grad_scores, queries[start:stop], preferred_element_type=F32)
            * score_scale
        )
    flat = (length_all, head_count * head_width)
    return (
        jnp.concatenate(grad_q).reshape(flat),
        grad_k.astype(BF).reshape(flat),
        grad_v.astype(BF).reshape(flat),
    )


def layer_forward(hidden_in, segment_ids, weights):
    w_attn, w_proj, w_hidden, w_back, attn_bias, hidden_bias, gains, shifts, head_width = weights
    width = w_proj.shape[1]
    normed_one, _, _ = norm_forward(hidden_in, gains[0], shifts[0])
    full_one = gather_rows(normed_one.astype(BF))
    length_all = full_one.shape[0]
    projected = dot(full_one, w_attn, ((1,), (0,)))

    def heads_of(values):
        return values.astype(BF).reshape(length_all, width // head_width, head_width)

    queries = heads_of(projected[:, :width] + attn_bias[0])
    key_rows = heads_of(projected[:, width : 2 * width])
    value_rows = heads_of(projected[:, 2 * width :] + attn_bias[1])
    mixed, logs = attend_forward(queries, key_rows, value_rows, segment_ids)
    branch = reduce_rows(dot(mixed, w_proj, ((1,), (1,))))
    after_attn = hidden_in + (branch + shifts[1])
    normed_two, _, _ = norm_forward(after_attn, gains[1], shifts[2])
    full_two = gather_rows(normed_two.astype(BF))
    pre_act = dot(full_two, w_hidden, ((1,), (0,))) + hidden_bias
    activated = jax.nn.gelu(pre_act, approximate=True).astype(BF)
    mlp_branch = reduce_rows(dot(activated, w_back, ((1,), (1,))))
    result = (after_attn + (mlp_branch + shifts[3])).astype(BF)
    kept = (
        hidden_in,
        full_one,
        queries,
        key_rows,
        value_rows,
        logs,
        mixed,
        after_attn,
        full_two,
        pre_act,
        activated,
    )
    return result, kept


def layer_backward(grad_out, kept, segment_ids, weights):
    w_attn, w_proj, w_hidden, w_back, attn_bias, hidden_bias, gains, shifts, head_width = weights
    (
        hidden_in,
        full_one,
        queries,
        key_rows,
        value_rows,
        logs,
        mixed,
        after_attn,
        full_two,
        pre_act,
        activated,
    ) = kept
    grad_mlp = grad_out.astype(BF)
    grad_out_bias = jnp.sum(grad_mlp.astype(F32), axis=0)
    full_grad_mlp = gather_rows(grad_mlp)
    grad_back = dot(full_grad_mlp, activated, ((0,), (0,)))
    grad_act = dot(full_grad_mlp, w_back, ((1,), (0,)))
    _, gelu_pull = jax.vjp(lambda inner: jax.nn.gelu(inner, approximate=True), pre_act)
    grad_pre = gelu_pull(grad_act)[0].astype(BF)
    grad_hidden_bias = jnp.sum(grad_pre.astype(F32), axis=0)
    grad_hidden = dot(full_two, grad_pre, ((0,), (0,)))
    grad_norm_two = reduce_rows(dot(grad_pre, w_hidden, ((1,), (1,))))
    _, normed, inverse = norm_forward(after_attn, gains[1], shifts[2])
    through, grad_gain_two, grad_shift_two = norm_backward(
        grad_norm_two, gains[1], normed, inverse
    )
    grad_mid = grad_out + through
    grad_attn = grad_mid.astype(BF)
    grad_proj_bias = jnp.sum(grad_attn.astype(F32), axis=0)
    full_grad_attn = gather_rows(grad_attn)
    grad_proj = dot(full_grad_attn, mixed, ((0,), (0,)))
    grad_mixed = dot(full_grad_attn, w_proj, ((1,), (0,))).astype(BF).reshape(queries.shape)
    grad_q, grad_k, grad_v = attend_backward(
        queries, key_rows, value_rows, segment_ids, logs, grad_mixed
    )
    grad_attn_bias = jnp.stack(
        [jnp.sum(grad_q.astype(F32), axis=0), jnp.sum(grad_v.astype(F32), axis=0)]
    )
    grad_qkv = jnp.concatenate([grad_q, grad_k, grad_v], axis=1)
    grad_attn_weight = dot(full_one, grad_qkv, ((0,), (0,)))
    grad_norm_one = reduce_rows(dot(grad_qkv, w_attn, ((1,), (1,))))
    _, normed, inverse = norm_forward(hidden_in, gains[0], shifts[0])
    through, grad_gain_one, grad_shift_one = norm_backward(
        grad_norm_one, gains[0], normed, inverse
    )
    grad_in = grad_mid + through
    matrices = jnp.concatenate(
        [
            grad_hidden.astype(BF),
            grad_back.astype(BF),
            grad_proj.astype(BF),
            grad_attn_weight.astype(BF),
        ],
        axis=1,
    )
    features = jnp.stack(
        [
            grad_gain_one,
            grad_gain_two,
            grad_shift_one,
            grad_proj_bias,
            grad_shift_two,
            grad_out_bias,
        ]
    )
    own_bias = jnp.concatenate([grad_attn_bias.reshape(-1), grad_hidden_bias])
    return grad_in, matrices, features, own_bias


def local(
    inputs, segments, w_qkv, qv_bias, w_out, w_up, up_bias, w_down, norm_gains, offsets, cotangent
):
    sections, cores, tensors = sizes()
    outers = lax.axis_size("outer")
    section = lax.axis_index("section")
    member = section * cores + lax.axis_index("core")
    replica = lax.axis_index("outer") * cores + lax.axis_index("core")
    replicas = outers * cores
    length_own, _, width = inputs.shape[1:]

    def own_micro(values):
        return lax.dynamic_index_in_dim(values, section, 0, keepdims=False)

    hidden = to_sequence(own_micro(inputs).reshape(length_own, width))
    segment_ids = to_sequence(own_micro(segments).reshape(-1))
    part_width = w_out.shape[1]
    small_parts = (norm_gains, offsets, qv_bias, up_bias)
    small = lax.all_gather(
        jnp.concatenate([part.reshape(-1) for part in small_parts]), EVERY, axis=0, tiled=False
    )
    small = small.reshape(sections, replicas, tensors, -1).astype(F32)
    first = to_sequence(
        jnp.concatenate([w_out[0].T, w_qkv[0].reshape(w_qkv.shape[1], -1)], axis=1)
    )
    second = to_sequence(jnp.concatenate([w_up[0], w_down[0].T], axis=1))

    def spread(block):
        gathered = lax.all_gather(block, REPLICAS, axis=0, tiled=False)
        gathered = gathered.reshape(outers, cores, sections, *block.shape)
        return [gathered[:, :, layer].reshape(-1, block.shape[1]) for layer in range(sections)]

    attn_sets = spread(first)
    mlp_sets = spread(second)
    heads_own, head_part = qv_bias.shape[2:]
    head_width = head_part * replicas
    hidden_own = w_up.shape[2]
    ends = []
    total = 0
    for part in small_parts:
        ends.append((total, total + part.size))
        total += part.size
    weights_all = []
    for layer in range(sections):
        rows = small[layer]
        gains = rows[:, :, ends[0][0] : ends[0][1]].reshape(-1, 2, norm_gains.shape[2])
        shifts = rows[:, :, ends[1][0] : ends[1][1]].reshape(-1, 4, offsets.shape[2])
        mine = lax.dynamic_index_in_dim(rows, member, 1, keepdims=False)
        attn_bias = mine[:, ends[2][0] : ends[2][1]].reshape(replicas, 2, heads_own, head_part)
        hidden_bias = mine[:, ends[3][0] : ends[3][1]].reshape(replicas, *up_bias.shape[1:])
        weights_all.append(
            (
                attn_sets[layer][:, part_width:],
                attn_sets[layer][:, :part_width],
                mlp_sets[layer][:, :hidden_own],
                mlp_sets[layer][:, hidden_own:],
                attn_bias.transpose(1, 2, 0, 3).reshape(2, -1),
                hidden_bias.transpose(1, 0, 2).reshape(-1),
                gains.transpose(1, 0, 2).reshape(2, -1),
                shifts.transpose(1, 0, 2).reshape(4, -1),
                head_width,
            )
        )
    grad = to_sequence(own_micro(cotangent).reshape(length_own, width)).astype(F32)
    kept_all = []
    outs = []
    for layer in range(sections):
        hidden, kept = layer_forward(hidden.astype(F32), segment_ids, weights_all[layer])
        kept_all.append(kept)
        outs.append(both_parts(hidden, layer))
    grads_in = [None] * sections
    matrix_sums = [None] * sections
    vector_sums = [None] * sections
    for layer in reversed(range(sections)):
        grad, matrices, features, own_bias = layer_backward(
            grad, kept_all[layer], segment_ids, weights_all[layer]
        )
        low = grad.astype(BF)
        grads_in[layer] = both_parts(low, layer)
        scattered = lax.psum_scatter(matrices, REPLICAS, scatter_dimension=0, tiled=True)
        matrix_sums[layer] = jnp.concatenate(both_parts(scattered, layer))
        placed = jnp.where(
            jnp.arange(tensors)[:, None] == member, own_bias[None], jnp.zeros((), F32)
        )
        vector_sums[layer] = lax.psum(
            jnp.concatenate([features.reshape(-1), placed.reshape(-1)]), EVERY
        )
        if layer:
            grad = low.astype(F32)

    def of_section(values):
        result = values[0]
        for layer in range(1, sections):
            result = jnp.where(section == layer, values[layer], result)
        return result

    layer_outputs = jnp.stack([of_section(pair) for pair in zip(*outs)])[None, :, :, None]
    input_grads = jnp.stack([of_section(pair) for pair in zip(*grads_in)]).astype(F32)
    matrix = of_section(matrix_sums).astype(F32)
    vector = of_section(vector_sums)
    features = vector[: 6 * width].reshape(6, width)
    feature_own = norm_gains.shape[2]
    features = lax.dynamic_slice_in_dim(
        features,
        (replica * tensors + lax.axis_index("tensor")) * feature_own,
        feature_own,
        1,
    )
    biases = lax.dynamic_index_in_dim(
        vector[6 * width :].reshape(tensors, -1), lax.axis_index("tensor"), 0, keepdims=False
    )
    attn_grads = biases[: 2 * part_width].reshape(2, heads_own, replicas, head_part)
    hidden_grads = biases[2 * part_width :].reshape(up_bias.shape[1], replicas, up_bias.shape[2])
    cut = 2 * hidden_own
    return (
        layer_outputs,
        input_grads[None, :, :, None],
        matrix[:, cut + part_width :].reshape(w_qkv.shape),
        lax.dynamic_index_in_dim(attn_grads, replica, 2, keepdims=False)[None],
        matrix[:, cut : cut + part_width].T[None],
        matrix[:, :hidden_own][None],
        lax.dynamic_index_in_dim(hidden_grads, replica, 1, keepdims=False)[None],
        matrix[:, hidden_own:cut].T[None],
        features[None, :2],
        features[None, 2:],
    )


def solution(mesh):
    sections, data, tensors = mesh.devices.shape
    fine = Mesh(mesh.devices.reshape(sections, data // 2, 2, tensors), EVERY)
    dp = ("outer", "core")
    every = ("outer", "core", "tensor")
    return jax.shard_map(
        local,
        mesh=fine,
        in_specs=(
            P(None, "tensor", dp, None),
            P(None, dp, None),
            P("section", dp, None, "tensor"),
            P("section", None, "tensor", dp),
            P("section", "tensor", dp),
            P("section", dp, "tensor"),
            P("section", "tensor", dp),
            P("section", "tensor", dp),
            P("section", None, every),
            P("section", None, every),
            P(None, "tensor", dp, None),
        ),
        out_specs=(
            P("section", None, "tensor", dp, None),
            P("section", None, "tensor", dp, None),
            P("section", dp, None, "tensor"),
            P("section", None, "tensor", dp),
            P("section", "tensor", dp),
            P("section", dp, "tensor"),
            P("section", "tensor", dp),
            P("section", "tensor", dp),
            P("section", None, every),
            P("section", None, every),
        ),
        check_vma=False,
    )
```
